32 devices in a mesh: proj: 8 (over z, y), grp: 4 (over x, core).
Axes of the slice: x: 2, y: 2, z: 4, core: 2. Of those that a mesh axis runs over, the one named last changes fastest.
Arguments:
- grads: bfloat16 [1024, 16384], P('grp', 'proj'), may hold values from -6 to 6
- proj_matrix: bfloat16 [16384, 8192], P('proj', 'grp'), may hold values from -48 to 48
- targets: bfloat16 [2048, 8192], P('proj', 'grp'), may hold values from -480 to 480
Outputs:
- scores: float32 [1024, 2048], P('proj', 'grp')
The draws below stay inside these ranges and needn't reach their ends.
All inputs are finite; a program needn't handle non-finite values.
Results may differ from the reference program's by a relative error of at most 0.0029.
Values may be sent and summed in bfloat16 or wider, within the bound.
No kernel may reach another device: no remote copies, remote signals or barrier semaphores. Data moves between devices by JAX's collectives and lax.ppermute only.
A program may use at most 128 MiB of HBM per device.

```python
import jax
import jax.numpy as jnp
from jax import lax

K = 8192
EX = 1024
TGT = 2048
P_SIZE = 16384


def column_scales(key):
    inner_key = jax.random.fold_in(key, 7)
    spread = jax.random.uniform(inner_key, (K,), jnp.float32, -1.15, 1.15)
    ramp = jnp.power(3.0, jnp.arange(K, dtype=jnp.float32) / K)
    return ramp * jnp.exp(spread)


def draw_proj_matrix(key, part):
    scales = column_scales(key)
    inner_key = jax.random.fold_in(key, 11)
    values = jnp.clip(jax.random.normal(inner_key, (P_SIZE, K), jnp.float32), -5.0, 5.0)
    return (values * scales[None, :]).astype(jnp.bfloat16)


def draw_targets(key, part):
    scales = column_scales(key)
    inner_key = jax.random.fold_in(key, 13)
    row_key = jax.random.fold_in(key, 17)
    row_scales = jnp.exp(jax.random.uniform(row_key, (TGT,), jnp.float32, 0.0, 2.3))
    values = jnp.clip(jax.random.normal(inner_key, (TGT, K), jnp.float32), -5.0, 5.0)
    return (values * scales[None, :] * row_scales[:, None]).astype(jnp.bfloat16)


def strengthened(array, stream_key, source, target, shards_of, factor):
    owner, partner = [(jnp.arange(array.shape[dim]) // (array.shape[dim] // shards_of)).reshape([-1 if axis == dim else 1 for axis in range(array.ndim)]) for dim in (source, target)]
    chosen = jax.random.permutation(stream_key, shards_of)[partner]
    strong = (owner == chosen) | (owner == (partner + shards_of // 2) % shards_of)
    return jnp.where(strong, factor * array, array)


def levels(stream_key, shape, cuts, smallest, high):
    def one(position, parts):
        steps = jax.random.uniform(jax.random.fold_in(jax.random.fold_in(stream_key, 6), position), (parts,), jnp.float32, smallest / len(cuts), high / len(cuts))
        return jnp.repeat(jnp.exp(steps), shape[position] // parts).reshape((-1,) + (1,) * (len(shape) - position - 1))

    gain = one(*cuts[0])
    for cut in cuts[1:]:
        gain = gain * one(*cut)
    return gain


def bell_draw_with(own_key, extent, width, most, shards, heavy, kind=jnp.bfloat16):
    values = width * jax.random.normal(own_key, extent, jnp.float32)
    if shards:
        values = values * levels(own_key, extent, shards, -0.22, 0.18)
    return jnp.clip(strengthened(values, jax.random.fold_in(own_key, 3), *heavy), -most, most).astype(kind)


def setup_inputs(seed: int = 0) -> dict:
    key_of = jax.random.split(jax.random.key(seed), 4)
    return {
        "grads": bell_draw_with(key_of[0], (EX, P_SIZE), 1.0, 6.0, ((0, 4), (1, 8)), (1, 0, 8, 2.0)),
        "proj_matrix": draw_proj_matrix(jax.random.fold_in(key_of[3], 71), 0),
        "targets": draw_targets(jax.random.fold_in(key_of[3], 71), 0),
    }


def reference(grads, proj_matrix, targets):
    features = jnp.dot(grads, proj_matrix, preferred_element_type=jnp.float32)
    rounded = features.astype(jnp.bfloat16)
    feature_sq = lax.optimization_barrier(jnp.sum(jnp.square(rounded.astype(jnp.float32)), axis=1))
    target_sq = lax.optimization_barrier(jnp.sum(jnp.square(targets.astype(jnp.float32)), axis=1))
    products = lax.dot_general(rounded, targets, (((1,), (1,)), ((), ())), preferred_element_type=jnp.float32)
    factor = float(K) ** 0.5
    return factor * products * lax.rsqrt(feature_sq + 1e-06)[:, None] * lax.rsqrt(target_sq + 1e-06)[None, :]
```

```python
import math

import jax
import jax.numpy as jnp
from jax import lax
from jax.sharding import PartitionSpec as P

F32, BF16, F16 = jnp.float32, jnp.bfloat16, jnp.float16
EPS = 1e-06


def swap(value, axis, size, bit):
    return lax.ppermute(value, axis, [(i, i ^ bit) for i in range(size)])


def inner_rows(left, right):
    return lax.dot_general(
        left, right, (((1,), (1,)), ((), ())), preferred_element_type=F32
    )


def pick(value, index, axis=0):
    return lax.dynamic_index_in_dim(value, index, axis, keepdims=False)


def per_device(n_p, n_g, grads, proj_matrix, targets):
    n_z = n_p // 2
    p, g = lax.axis_index("proj"), lax.axis_index("grp")
    py, pz = p % 2, p // 2
    rows, depth = grads.shape
    width = proj_matrix.shape[1]
    tgt_rows = targets.shape[0]
    examples = rows * n_g
    own = examples // n_p
    piece = width // n_z
    half = rows // 2

    def over_z(block_of, bit):
        return swap(block_of(pz ^ bit), "proj", n_p, 2 * bit)

    grads_1 = swap(grads, "grp", n_g, 1)
    grads_2 = swap(grads, "grp", n_g, 2)
    grads_3 = swap(grads_2, "grp", n_g, 1)
    chunks = [grads, grads_1, grads_2, grads_3]

    def target_piece(z):
        return lax.dynamic_slice_in_dim(targets, z * piece, piece, 1)

    tgt = [target_piece(pz)] + [over_z(target_piece, bit) for bit in range(1, n_z)]

    row_max = jnp.max(jnp.abs(grads), axis=1).astype(F32) * jnp.max(jnp.abs(proj_matrix)).astype(F32)
    tgt_sq = jnp.sum(jnp.square(targets.astype(F32)), axis=1)
    row_max = lax.dynamic_update_slice_in_dim(jnp.zeros((examples,), F32), row_max, g * rows, 0)
    tgt_sq = lax.dynamic_update_slice_in_dim(jnp.zeros((tgt_rows * n_p,), F32), tgt_sq, p * tgt_rows, 0)
    steps = [("grp", n_g, 1 << k) for k in range(int(math.log2(n_g)))]
    steps += [("proj", n_p, 1 << k) for k in range(int(math.log2(n_p)))]
    for step in steps:
        both = swap(jnp.concatenate([row_max, tgt_sq]), *step)
        row_max = jnp.maximum(row_max, both[:examples])
        tgt_sq = tgt_sq + both[examples:]
    bound = row_max * float(depth * n_p)
    scale = jnp.exp2(jnp.clip(15.0 - jnp.ceil(jnp.log2(jnp.maximum(bound, 1e-30))), -40.0, 60.0))
    tgt_norm = lax.rsqrt(tgt_sq + EPS)

    def side(value, y):
        shape = (rows // (2 * own), 2, own) + value.shape[1:]
        return pick(value.reshape(shape), y, 1).reshape((half,) + value.shape[1:])

    def features_of(i, chunk):
        rows_scale = lax.dynamic_slice_in_dim(scale, (g ^ i) * rows, rows, 0)
        keep_scale = side(rows_scale, py)[:, None]
        part = jnp.dot(side(chunk, 1 - py), proj_matrix, preferred_element_type=F32)
        if i < 2:
            got = swap(part.astype(BF16), "proj", n_p, 1).astype(F32)
        else:
            send_scale = side(rows_scale, 1 - py)[:, None]
            got = swap((part * send_scale).astype(F16), "proj", n_p, 1).astype(F32)
        part = jnp.dot(side(chunk, py), proj_matrix, preferred_element_type=F32)
        part = (part + got) * keep_scale if i < 2 else part * keep_scale + got

        def block_of(z):
            return lax.dynamic_slice_in_dim(part, z * piece, piece, 1)

        total = block_of(pz)
        for bit in range(1, n_z):
            total = total + over_z(lambda z: block_of(z).astype(F16), bit).astype(F32)
        return total.astype(BF16)

    features = [features_of(i, chunk) for i, chunk in enumerate(chunks)]
    features = jnp.stack(features)
    features = jnp.concatenate([pick(features, b ^ g) for b in range(n_g)])
    feature_sq = jnp.sum(jnp.square(features.astype(F32)), axis=1)

    tgt = jnp.stack(tgt)
    other = swap(tgt, "proj", n_p, 1)
    pair = [jnp.where(py == 0, tgt, other), jnp.where(py == 0, other, tgt)]
    tgt = jnp.stack(pair, axis=1)
    tgt = jnp.stack([pick(tgt, pz ^ b) for b in range(n_z)])
    tgt = tgt.reshape(n_g, tgt_rows * n_p // n_g, piece)
    tgt_norm = tgt_norm.reshape(n_g, -1)

    def products_of(q):
        return inner_rows(features, pick(tgt, g ^ q))

    own_part = products_of(0) + swap(products_of(1), "grp", n_g, 1)
    far_part = products_of(2) + swap(products_of(3), "grp", n_g, 1)
    norm = [pick(tgt_norm, g ^ q)[None, :] / 64.0 for q in (0, 2)]
    part = own_part * norm[0] + swap((far_part * norm[1]).astype(F16), "grp", n_g, 2).astype(F32)

    part = part.reshape(n_z, own, -1)
    total = pick(part, pz)
    for bit in range(1, n_z):
        total = total + over_z(lambda z: pick(part, z).astype(F16), bit).astype(F32)

    for k in range(2):
        feature_sq = feature_sq + swap(feature_sq, "grp", n_g, 1 << k)
    for k in range(1, int(math.log2(n_p))):
        feature_sq = feature_sq + swap(feature_sq, "proj", n_p, 1 << k)
    feature_sq = pick(feature_sq.reshape(n_z, own), pz)
    own_scale = lax.dynamic_slice_in_dim(scale, p * own, own, 0)
    factor = 64.0 * float(width * n_g) ** 0.5
    return factor * total * lax.rsqrt(feature_sq + EPS * own_scale * own_scale)[:, None]


def solution(mesh):
    n_p, n_g = mesh.shape["proj"], mesh.shape["grp"]

    def body(grads, proj_matrix, targets):
        return per_device(n_p, n_g, grads, proj_matrix, targets)

    placed = (P("grp", "proj"), P("proj", "grp"), P("proj", "grp"))
    return jax.shard_map(
        body, mesh=mesh, in_specs=placed, out_specs=P("proj", "grp"), check_vma=False
    )
```

```python
import math

import jax
import jax.numpy as jnp
from jax import lax
from jax.sharding import PartitionSpec as P

F32, BF16, F16 = jnp.float32, jnp.bfloat16, jnp.float16
EPS = 1e-06


def swap(value, axis, size, bit):
    return lax.ppermute(value, axis, [(i, i ^ bit) for i in range(size)])


def inner_rows(left, right):
    return lax.dot_general(
        left, right, (((1,), (1,)), ((), ())), preferred_element_type=F32
    )


def pick(value, index, axis=0):
    return lax.dynamic_index_in_dim(value, index, axis, keepdims=False)


def after(value, earlier):
    cols, width = value.shape[-1], earlier.shape[-1]
    row = earlier[(0,) * (earlier.ndim - 1)]
    row = jnp.tile(row, cols // width) if cols > width else row[:cols]
    return value + (0.0 * row.astype(F32)).astype(value.dtype)


def encode(value, gain):
    return (value * (lax.rsqrt(jnp.maximum(jnp.abs(value), 1e-35)) * gain)).astype(F16)


def decode(code, gain):
    code = code.astype(F32)
    return code * jnp.abs(code) * (1.0 / (gain * gain))


MOST_GRAD, MOST_PROJ, MOST_TARGET = 16.0, 48.0, 480.0
NORM_GAIN = 0.5


def gain_for(most):
    return 2.0 ** math.floor(15.99 - 0.5 * math.log2(most))


def per_device(n_p, n_g, grads, proj_matrix, targets):
    n_z = n_p // 2
    p, g = lax.axis_index("proj"), lax.axis_index("grp")
    py, pz = p % 2, p // 2
    rows = grads.shape[0]
    width = proj_matrix.shape[1]
    tgt_rows = targets.shape[0]
    own = rows * n_g // n_p
    piece = width // n_z
    half = rows // 2

    most_feature = grads.shape[1] * n_p * MOST_GRAD * MOST_PROJ
    feature_gain = gain_for(most_feature)
    product_gain = gain_for(most_feature * MOST_TARGET * piece * n_g)

    z_bits = [1 << k for k in range(n_z.bit_length() - 1)]

    def reversed_bits(z):
        return sum(((z >> k) & 1) << (len(z_bits) - 1 - k) for k in range(len(z_bits)))

    last, flags = [None], {"gate": True, "mark": True}

    def then(value):
        return value if last[0] is None or not flags["gate"] else after(value, last[0])

    def done(value):
        if flags["mark"]:
            last[0] = value
        return value

    def step(work, *args, gate=True, mark=True):
        flags.update(gate=gate, mark=mark)
        return work(*args)

    def side(value, y):
        shape = (rows // (2 * own), 2, own) + value.shape[1:]
        return pick(value.reshape(shape), y, 1).reshape((half,) + value.shape[1:])

    order = sorted(range(n_z), key=lambda k: [k & bit for bit in z_bits])


    def columns(value):
        return jnp.stack([lax.dynamic_slice_in_dim(value, (pz ^ k) * piece, piece, 1) for k in order])

    kept, code, features = {}, {}, {}

    def partial(i, chunk):
        part = done(jnp.dot(then(chunk), proj_matrix, preferred_element_type=F32))
        kept[i] = side(part, py)
        code[i] = swap(encode(side(part, 1 - py), feature_gain), "proj", n_p, 1)

    def partial_away(i, chunk):
        part = done(jnp.dot(then(side(chunk, 1 - py)), proj_matrix, preferred_element_type=F32))
        code[i] = swap(encode(part, feature_gain), "proj", n_p, 1)

    def partial_kept(i, chunk):
        kept[i] = done(jnp.dot(then(side(chunk, py)), proj_matrix, preferred_element_type=F32))

    def collect(i):
        return done(then(kept[i]) + decode(code[i], feature_gain))

    def spread(i, bit):
        part = collect(i)
        part = columns(part) if bit == 1 else part
        kept[i], away = jnp.split(part, 2)
        code[i] = swap(encode(away, feature_gain), "proj", n_p, 2 * bit)

    def finish(i):
        features[i] = collect(i)[0].astype(BF16)

    def targets_over_z(blocks, bit):
        blocks = then(blocks)
        low, high = jnp.split(blocks, 2, axis=2)
        upper = (pz // bit) % 2 == 1
        return jnp.where(upper, high, low), swap(jnp.where(upper, low, high), "proj", n_p, 2 * bit)

    def joined(keep, got):
        return done(jnp.concatenate([keep, then(got)]))

    grads_2 = swap(grads, "grp", n_g, 2)
    grads_1 = swap(grads, "grp", n_g, 1)

    step(partial, 0, grads)
    grads_3 = swap(grads_2, "grp", n_g, 1)
    tgt = step(targets_over_z, targets[None], z_bits[-1])
    step(partial, 1, grads_1)
    step(spread, 0, 1)
    step(partial_away, 2, grads_2)
    step(spread, 1, 1)
    step(partial_kept, 2, grads_2)
    for bit in z_bits[-2::-1]:
        tgt = step(targets_over_z, step(joined, *tgt), bit, gate=False)
    step(partial_away, 3, grads_3)
    step(partial_kept, 3, grads_3)
    step(spread, 2, 1)
    for bit in z_bits[1:]:
        step(spread, 0, bit, mark=False)
    tgt = step(joined, *tgt)
    other = swap(tgt, "proj", n_p, 1)
    for bit in z_bits[1:]:
        step(spread, 1, bit)
    step(finish, 0)
    step(spread, 3, 1, gate=False)
    for bit in z_bits[1:]:
        step(spread, 2, bit, gate=False)
    step(finish, 1)
    for bit in z_bits[1:]:
        step(spread, 3, bit)
    step(finish, 2)
    step(finish, 3)

    in_chunk = n_z // n_g

    def row_block(z):
        return pick(features, ((z // in_chunk) ^ g) * in_chunk + z % in_chunk)

    features = jnp.stack([features[i] for i in range(n_g)]).reshape(n_z, own, piece)
    features = jnp.stack([row_block(pz ^ k) for k in range(n_z)])
    feature_sq = jnp.sum(jnp.square(features.astype(F32)), axis=2)
    features = features.reshape(n_z * own, piece)

    def of_member(q, mine, partners):
        places = [reversed_bits(pz ^ ((g ^ q) * in_chunk + n)) for n in range(in_chunk)]
        return jnp.concatenate([pick(value, at) for at in places for value in (mine, partners)])

    def products_of(q):
        return inner_rows(features, of_member(q, tgt, other)).reshape(n_z, own, -1)

    far, near = slice(1, n_z), slice(0, 1)
    prods = {3: products_of(3)}
    got_3 = swap(done(prods[3]), "grp", n_g, 1)
    prods[2] = products_of(2)
    prods[1] = products_of(1)
    got_1 = swap(then(prods[1]), "grp", n_g, 1)
    prods[0] = products_of(0)
    far_part = prods[2] + got_3
    own_part = prods[0] + got_1

    tgt_sq = [jnp.sum(jnp.square(value.astype(F32)), axis=2) for value in (tgt, other)]
    tgt_sq = jnp.stack([of_member(q, *tgt_sq) for q in range(n_g)])
    cols = tgt_sq.shape[1]
    got = swap(jnp.concatenate([feature_sq.reshape(-1), tgt_sq[1], tgt_sq[3]]), "grp", n_g, 1)
    feature_sq = feature_sq + got[: n_z * own].reshape(n_z, own)
    tgt_sq = [tgt_sq[2 * n] + got[n_z * own + n * cols :][:cols] for n in range(2)]

    def norm_rows(feature_sq, tgt_sq):
        rows = jnp.concatenate([jnp.pad(feature_sq, ((0, 0), (0, cols - own))), tgt_sq[None]])
        return jnp.pad(rows, ((0, -rows.shape[0] % 16), (0, 0)))

    def coded(product, norms):
        return jnp.concatenate([encode(product, product_gain), encode(jnp.sqrt(norms), NORM_GAIN)])

    def decoded(code, rows):
        product, norms = jnp.split(code, [rows])
        return decode(product, product_gain), jnp.square(decode(norms, NORM_GAIN))

    far_rows = (n_z - 1) * own
    codes = [swap(coded(far_part[far].reshape(far_rows, cols), norm_rows(feature_sq, tgt_sq[1])), "grp", n_g, 2)]
    codes.append(swap(encode(far_part[near][0], product_gain), "grp", n_g, 2))
    got, got_norms = decoded(codes[0], far_rows)
    part = done(then(own_part[far]) + got.reshape(n_z - 1, own, cols))
    feature_sq = feature_sq + got_norms[:n_z, :own]
    tgt_sq = tgt_sq[0] + got_norms[n_z]

    norms = [norm_rows(feature_sq[k : k + 1], tgt_sq) for k in range(n_z)]
    sends = [swap(coded(part[k - 1], norms[k]), "proj", n_p, 2 * k) for k in range(1, n_z)]
    total = then(own_part[near])[0] + decode(codes[1], product_gain)
    norms = norms[0]
    for code in sends:
        got, got_norms = decoded(code, own)
        total, norms = total + got, norms + got_norms

    factor = float(width * n_g) ** 0.5
    scores = factor * total * lax.rsqrt(norms[0, :own] + EPS)[:, None] * lax.rsqrt(norms[1] + EPS)[None, :]
    blocks = jnp.split(scores, 2 * in_chunk, axis=1)
    swapped = jnp.concatenate([blocks[n ^ 1] for n in range(2 * in_chunk)], axis=1)
    return jnp.where(py == 0, scores, swapped)


def solution(mesh):
    n_p, n_g = mesh.shape["proj"], mesh.shape["grp"]

    def body(grads, proj_matrix, targets):
        return per_device(n_p, n_g, grads, proj_matrix, targets)

    placed = (P("grp", "proj"), P("proj", "grp"), P("proj", "grp"))
    return jax.shard_map(
        body, mesh=mesh, in_specs=placed, out_specs=P("proj", "grp"), check_vma=False
    )
```

```python
import math

import jax
import jax.numpy as jnp
from jax import lax
from jax.sharding import PartitionSpec as P

F32, BF16, F16 = jnp.float32, jnp.bfloat16, jnp.float16
EPS = 1e-06


def swap(value, axis, size, bit):
    return lax.ppermute(value, axis, [(i, i ^ bit) for i in range(size)])


def inner_rows(left, right):
    return lax.dot_general(
        left, right, (((1,), (1,)), ((), ())), preferred_element_type=F32
    )


def pick(value, index, axis=0):
    return lax.dynamic_index_in_dim(value, index, axis, keepdims=False)


def after(value, earlier):
    cols, width = value.shape[-1], earlier.shape[-1]
    row = earlier[(0,) * (earlier.ndim - 1)]
    row = jnp.tile(row, cols // width) if cols > width else row[:cols]
    return value + (0.0 * row.astype(F32)).astype(value.dtype)


def encode(value, gain):
    return (value * (lax.rsqrt(jnp.maximum(jnp.abs(value), 1e-35)) * gain)).astype(F16)


def decode(code, gain):
    code = code.astype(F32)
    return code * jnp.abs(code) * (1.0 / (gain * gain))


MOST_GRAD, MOST_PROJ, MOST_TARGET = 16.0, 48.0, 480.0
NORM_GAIN = 0.5


def gain_for(most):
    return 2.0 ** math.floor(15.99 - 0.5 * math.log2(most))


def per_device(n_p, n_g, grads, proj_matrix, targets):
    n_z = n_p // 2
    p, g = lax.axis_index("proj"), lax.axis_index("grp")
    py, pz = p % 2, p // 2
    rows = grads.shape[0]
    width = proj_matrix.shape[1]
    tgt_rows = targets.shape[0]
    own = rows * n_g // n_p
    piece = width // n_z
    half = rows // 2

    most_feature = grads.shape[1] * n_p * MOST_GRAD * MOST_PROJ
    feature_gain = gain_for(most_feature)
    product_gain = gain_for(most_feature * MOST_TARGET * piece * n_g)

    z_bits = [1 << k for k in range(n_z.bit_length() - 1)]

    def reversed_bits(z):
        return sum(((z >> k) & 1) << (len(z_bits) - 1 - k) for k in range(len(z_bits)))

    last, flags = [None], {"gate": True, "mark": True}

    def then(value):
        return value if last[0] is None or not flags["gate"] else after(value, last[0])

    def done(value):
        if flags["mark"]:
            last[0] = value
        return value

    def step(work, *args, gate=True, mark=True):
        flags.update(gate=gate, mark=mark)
        return work(*args)

    def side(value, y):
        shape = (rows // (2 * own), 2, own) + value.shape[1:]
        return pick(value.reshape(shape), y, 1).reshape((half,) + value.shape[1:])

    order = sorted(range(n_z), key=lambda k: [k & bit for bit in z_bits])


    def columns(value):
        return jnp.stack([lax.dynamic_slice_in_dim(value, (pz ^ k) * piece, piece, 1) for k in order])

    kept, code, features = {}, {}, {}

    def partial_away(i, chunk):
        part = done(jnp.dot(then(side(chunk, 1 - py)), proj_matrix, preferred_element_type=F32))
        code[i] = swap(encode(part, feature_gain), "proj", n_p, 1)

    def partial_kept(i, chunk):
        kept[i] = done(jnp.dot(then(side(chunk, py)), proj_matrix, preferred_element_type=F32))

    def collect(i):
        return done(then(kept[i]) + decode(code[i], feature_gain))

    def spread(i, bit):
        part = collect(i)
        part = columns(part) if bit == 1 else part
        kept[i], away = jnp.split(part, 2)
        code[i] = swap(encode(away, feature_gain), "proj", n_p, 2 * bit)

    def finish(i):
        features[i] = collect(i)[0].astype(BF16)

    def targets_over_z(blocks, bit):
        blocks = then(blocks)
        low, high = jnp.split(blocks, 2, axis=2)
        upper = (pz // bit) % 2 == 1
        return jnp.where(upper, high, low), swap(jnp.where(upper, low, high), "proj", n_p, 2 * bit)

    def joined(keep, got):
        return done(jnp.concatenate([keep, then(got)]))

    grads_2 = swap(grads, "grp", n_g, 2)
    grads_1 = swap(grads, "grp", n_g, 1)

    step(partial_away, 0, grads)
    grads_3 = swap(grads_2, "grp", n_g, 1)
    tgt = step(targets_over_z, targets[None], z_bits[-1])
    step(partial_away, 1, grads_1)
    step(partial_kept, 0, grads)
    step(spread, 0, 1)
    step(partial_kept, 1, grads_1)
    step(partial_away, 2, grads_2)
    step(spread, 1, 1)
    step(partial_kept, 2, grads_2)
    for bit in z_bits[-2::-1]:
        tgt = step(targets_over_z, step(joined, *tgt), bit, gate=False)
    step(partial_away, 3, grads_3)
    step(partial_kept, 3, grads_3)
    step(spread, 2, 1)
    for bit in z_bits[1:]:
        step(spread, 0, bit, mark=False)
    tgt = step(joined, *tgt)
    other = swap(tgt, "proj", n_p, 1)
    for bit in z_bits[1:]:
        step(spread, 1, bit)
    step(finish, 0)
    step(spread, 3, 1, gate=False)
    for bit in z_bits[1:]:
        step(spread, 2, bit, gate=False)
    step(finish, 1)
    for bit in z_bits[1:]:
        step(spread, 3, bit)
    step(finish, 2)
    step(finish, 3)

    in_chunk = n_z // n_g

    def row_block(z):
        return pick(features, ((z // in_chunk) ^ g) * in_chunk + z % in_chunk)

    features = jnp.stack([features[i] for i in range(n_g)]).reshape(n_z, own, piece)
    features = jnp.stack([row_block(pz ^ k) for k in range(n_z)])
    feature_sq = jnp.sum(jnp.square(features.astype(F32)), axis=2)
    features = features.reshape(n_z * own, piece)

    def of_member(q, mine, partners):
        places = [reversed_bits(pz ^ ((g ^ q) * in_chunk + n)) for n in range(in_chunk)]
        return jnp.concatenate([pick(value, at) for at in places for value in (mine, partners)])

    def products_of(q):
        return inner_rows(features, of_member(q, tgt, other)).reshape(n_z, own, -1)

    far, near = slice(1, n_z), slice(0, 1)
    prods = {3: products_of(3)}
    got_3 = swap(done(prods[3]), "grp", n_g, 1)
    prods[2] = products_of(2)
    prods[1] = products_of(1)
    got_1 = swap(then(prods[1]), "grp", n_g, 1)
    prods[0] = products_of(0)
    far_part = prods[2] + got_3
    own_part = prods[0] + got_1

    tgt_sq = [jnp.sum(jnp.square(value.astype(F32)), axis=2) for value in (tgt, other)]
    tgt_sq = jnp.stack([of_member(q, *tgt_sq) for q in range(n_g)])
    cols = tgt_sq.shape[1]
    got = swap(jnp.concatenate([feature_sq.reshape(-1), tgt_sq[1], tgt_sq[3]]), "grp", n_g, 1)
    feature_sq = feature_sq + got[: n_z * own].reshape(n_z, own)
    tgt_sq = [tgt_sq[2 * n] + got[n_z * own + n * cols :][:cols] for n in range(2)]

    def norm_rows(feature_sq, tgt_sq):
        rows = jnp.concatenate([jnp.pad(feature_sq, ((0, 0), (0, cols - own))), tgt_sq[None]])
        return jnp.pad(rows, ((0, -rows.shape[0] % 16), (0, 0)))

    def coded(product, norms):
        return jnp.concatenate([encode(product, product_gain), encode(jnp.sqrt(norms), NORM_GAIN)])

    def decoded(code, rows):
        product, norms = jnp.split(code, [rows])
        return decode(product, product_gain), jnp.square(decode(norms, NORM_GAIN))

    far_rows = (n_z - 1) * own
    codes = [swap(coded(far_part[far].reshape(far_rows, cols), norm_rows(feature_sq, tgt_sq[1])), "grp", n_g, 2)]
    codes.append(swap(encode(far_part[near][0], product_gain), "grp", n_g, 2))
    got, got_norms = decoded(codes[0], far_rows)
    part = done(then(own_part[far]) + got.reshape(n_z - 1, own, cols))
    feature_sq = feature_sq + got_norms[:n_z, :own]
    tgt_sq = tgt_sq[0] + got_norms[n_z]

    norms = [norm_rows(feature_sq[k : k + 1], tgt_sq) for k in range(n_z)]
    sends = [swap(coded(part[k - 1], norms[k]), "proj", n_p, 2 * k) for k in range(1, n_z)]
    total = then(own_part[near])[0] + decode(codes[1], product_gain)
    norms = norms[0]
    for code in sends:
        got, got_norms = decoded(code, own)
        total, norms = total + got, norms + got_norms

    factor = float(width * n_g) ** 0.5
    scores = factor * total * lax.rsqrt(norms[0, :own] + EPS)[:, None] * lax.rsqrt(norms[1] + EPS)[None, :]
    blocks = jnp.split(scores, 2 * in_chunk, axis=1)
    swapped = jnp.concatenate([blocks[n ^ 1] for n in range(2 * in_chunk)], axis=1)
    return jnp.where(py == 0, scores, swapped)


def solution(mesh):
    n_p, n_g = mesh.shape["proj"], mesh.shape["grp"]

    def body(grads, proj_matrix, targets):
        return per_device(n_p, n_g, grads, proj_matrix, targets)

    placed = (P("grp", "proj"), P("proj", "grp"), P("proj", "grp"))
    return jax.shard_map(
        body, mesh=mesh, in_specs=placed, out_specs=P("proj", "grp"), check_vma=False
    )
```

```python
import math

import jax
import jax.numpy as jnp
from jax import lax
from jax.sharding import PartitionSpec as P

F32, BF16, F16 = jnp.float32, jnp.bfloat16, jnp.float16
EPS = 1e-06


def swap(value, axis, size, bit):
    return lax.ppermute(value, axis, [(i, i ^ bit) for i in range(size)])


def inner_rows(left, right):
    return lax.dot_general(
        left, right, (((1,), (1,)), ((), ())), preferred_element_type=F32
    )


def pick(value, index, axis=0):
    return lax.dynamic_index_in_dim(value, index, axis, keepdims=False)


def after(value, earlier):
    cols, width = value.shape[-1], earlier.shape[-1]
    row = earlier[(0,) * (earlier.ndim - 1)]
    row = jnp.tile(row, cols // width) if cols > width else row[:cols]
    return value + (0.0 * row.astype(F32)).astype(value.dtype)


def encode(value, gain):
    return (value * (lax.rsqrt(jnp.maximum(jnp.abs(value), 1e-35)) * gain)).astype(F16)


def decode(code, gain):
    code = code.astype(F32)
    return code * jnp.abs(code) * (1.0 / (gain * gain))


MOST_GRAD, MOST_PROJ, MOST_TARGET = 16.0, 48.0, 480.0
NORM_GAIN = 0.5


def gain_for(most):
    return 2.0 ** math.floor(15.99 - 0.5 * math.log2(most))


def per_device(n_p, n_g, grads, proj_matrix, targets):
    n_z = n_p // 2
    p, g = lax.axis_index("proj"), lax.axis_index("grp")
    py, pz = p % 2, p // 2
    rows = grads.shape[0]
    width = proj_matrix.shape[1]
    tgt_rows = targets.shape[0]
    own = rows * n_g // n_p
    piece = width // n_z
    half = rows // 2

    most_feature = grads.shape[1] * n_p * MOST_GRAD * MOST_PROJ
    feature_gain = gain_for(most_feature)
    product_gain = gain_for(most_feature * MOST_TARGET * piece * n_g)

    z_bits = [1 << k for k in range(n_z.bit_length() - 1)]

    def reversed_bits(z):
        return sum(((z >> k) & 1) << (len(z_bits) - 1 - k) for k in range(len(z_bits)))

    last, flags = [None], {"gate": True, "mark": True}

    def then(value):
        return value if last[0] is None or not flags["gate"] else after(value, last[0])

    def done(value):
        if flags["mark"]:
            last[0] = value
        return value

    def step(work, *args, gate=True, mark=True):
        flags.update(gate=gate, mark=mark)
        return work(*args)

    def side(value, y):
        shape = (rows // (2 * own), 2, own) + value.shape[1:]
        return pick(value.reshape(shape), y, 1).reshape((half,) + value.shape[1:])

    order = sorted(range(n_z), key=lambda k: [k & bit for bit in z_bits])


    def columns(value):
        return jnp.stack([lax.dynamic_slice_in_dim(value, (pz ^ k) * piece, piece, 1) for k in order])

    kept, code, features = {}, {}, {}

    def partial_away(i, chunk):
        part = done(jnp.dot(then(side(chunk, 1 - py)), proj_matrix, preferred_element_type=F32))
        code[i] = swap(encode(part, feature_gain), "proj", n_p, 1)

    def partial_kept(i, chunk):
        kept[i] = done(jnp.dot(then(side(chunk, py)), proj_matrix, preferred_element_type=F32))

    def collect(i):
        return done(then(kept[i]) + decode(code[i], feature_gain))

    def spread(i, bit):
        part = collect(i)
        part = columns(part) if bit == 1 else part
        kept[i], away = jnp.split(part, 2)
        code[i] = swap(encode(away, feature_gain), "proj", n_p, 2 * bit)

    def finish(i):
        features[i] = collect(i)[0].astype(BF16)

    def targets_over_z(blocks, bit):
        blocks = then(blocks)
        low, high = jnp.split(blocks, 2, axis=2)
        upper = (pz // bit) % 2 == 1
        return jnp.where(upper, high, low), swap(jnp.where(upper, low, high), "proj", n_p, 2 * bit)

    def joined(keep, got):
        return done(jnp.concatenate([keep, then(got)]))

    grads_2 = swap(grads, "grp", n_g, 2)
    grads_1 = swap(grads, "grp", n_g, 1)

    step(partial_away, 0, grads)
    grads_3 = swap(grads_2, "grp", n_g, 1)
    tgt = step(targets_over_z, targets[None], z_bits[-1])
    step(partial_away, 1, grads_1)
    step(partial_kept, 0, grads)
    step(spread, 0, 1)
    step(partial_kept, 1, grads_1)
    step(partial_away, 2, grads_2)
    step(spread, 1, 1)
    step(partial_kept, 2, grads_2)
    for bit in z_bits[-2::-1]:
        tgt = step(targets_over_z, step(joined, *tgt), bit, gate=False)
    step(partial_away, 3, grads_3)
    step(partial_kept, 3, grads_3)
    step(spread, 2, 1)
    for bit in z_bits[1:]:
        step(spread, 0, bit, mark=False)
    tgt = step(joined, *tgt)
    other = swap(tgt, "proj", n_p, 1)
    for bit in z_bits[1:]:
        step(spread, 1, bit)
    step(finish, 0)
    step(spread, 3, 1, gate=False)
    for bit in z_bits[1:]:
        step(spread, 2, bit, gate=False)
    step(finish, 1)
    for bit in z_bits[1:]:
        step(spread, 3, bit)
    step(finish, 2)
    step(finish, 3)

    in_chunk = n_z // n_g

    def row_block(z):
        return pick(features, ((z // in_chunk) ^ g) * in_chunk + z % in_chunk)

    features = jnp.stack([features[i] for i in range(n_g)]).reshape(n_z, own, piece)
    features = jnp.stack([row_block(pz ^ k) for k in range(n_z)])
    feature_sq = jnp.sum(jnp.square(features.astype(F32)), axis=2)
    features = features.reshape(n_z * own, piece)

    def of_member(q, mine, partners):
        places = [reversed_bits(pz ^ ((g ^ q) * in_chunk + n)) for n in range(in_chunk)]
        return jnp.concatenate([pick(value, at) for at in places for value in (mine, partners)])

    def products_of(q):
        return inner_rows(features, of_member(q, tgt, other)).reshape(n_z, own, -1)

    far, near = slice(1, n_z), slice(0, 1)
    prods = {3: products_of(3)}
    got_3 = swap(done(prods[3]), "grp", n_g, 1)
    prods[2] = products_of(2)
    prods[1] = products_of(1)
    got_1 = swap(then(prods[1]), "grp", n_g, 1)
    prods[0] = products_of(0)
    far_part = prods[2] + got_3
    own_part = prods[0] + got_1

    tgt_sq = [jnp.sum(jnp.square(value.astype(F32)), axis=2) for value in (tgt, other)]
    tgt_sq = jnp.stack([of_member(q, *tgt_sq) for q in range(n_g)])
    cols = tgt_sq.shape[1]
    got = swap(jnp.concatenate([feature_sq.reshape(-1), tgt_sq[1], tgt_sq[3]]), "grp", n_g, 1)
    feature_sq = feature_sq + got[: n_z * own].reshape(n_z, own)
    tgt_sq = [tgt_sq[2 * n] + got[n_z * own + n * cols :][:cols] for n in range(2)]

    def norm_rows(feature_sq, tgt_sq):
        rows = jnp.concatenate([jnp.pad(feature_sq, ((0, 0), (0, cols - own))), tgt_sq[None]])
        return jnp.pad(rows, ((0, -rows.shape[0] % 8), (0, 0)))

    def coded(product, norms):
        return jnp.concatenate([encode(product, product_gain), encode(jnp.sqrt(norms), NORM_GAIN)])

    def decoded(code, rows):
        product, norms = jnp.split(code, [rows])
        return decode(product, product_gain), jnp.square(decode(norms, NORM_GAIN))

    far_rows = (n_z - 1) * own
    codes = [swap(coded(far_part[far].reshape(far_rows, cols), norm_rows(feature_sq, tgt_sq[1])), "grp", n_g, 2)]
    codes.append(swap(encode(far_part[near][0], product_gain), "grp", n_g, 2))
    got, got_norms = decoded(codes[0], far_rows)
    part = done(then(own_part[far]) + got.reshape(n_z - 1, own, cols))
    feature_sq = feature_sq + got_norms[:n_z, :own]
    tgt_sq = tgt_sq[0] + got_norms[n_z]

    norms = [norm_rows(feature_sq[k : k + 1], tgt_sq) for k in range(n_z)]
    sends = [swap(coded(part[k - 1], norms[k]), "proj", n_p, 2 * k) for k in range(1, n_z)]
    total = then(own_part[near])[0] + decode(codes[1], product_gain)
    norms = norms[0]
    for code in sends:
        got, got_norms = decoded(code, own)
        total, norms = total + got, norms + got_norms

    factor = float(width * n_g) ** 0.5
    scores = factor * total * lax.rsqrt(norms[0, :own] + EPS)[:, None] * lax.rsqrt(norms[1] + EPS)[None, :]
    blocks = jnp.split(scores, 2 * in_chunk, axis=1)
    swapped = jnp.concatenate([blocks[n ^ 1] for n in range(2 * in_chunk)], axis=1)
    return jnp.where(py == 0, scores, swapped)


def solution(mesh):
    n_p, n_g = mesh.shape["proj"], mesh.shape["grp"]

    def body(grads, proj_matrix, targets):
        return per_device(n_p, n_g, grads, proj_matrix, targets)

    placed = (P("grp", "proj"), P("proj", "grp"), P("proj", "grp"))
    return jax.shard_map(
        body, mesh=mesh, in_specs=placed, out_specs=P("proj", "grp"), check_vma=False
    )
```

```python
import math

import jax
import jax.numpy as jnp
from jax import lax
from jax.sharding import PartitionSpec as P

F32, BF16, F16 = jnp.float32, jnp.bfloat16, jnp.float16
EPS = 1e-06


def swap(value, axis, size, bit):
    return lax.ppermute(value, axis, [(i, i ^ bit) for i in range(size)])


def inner_rows(left, right):
    return lax.dot_general(
        left, right, (((1,), (1,)), ((), ())), preferred_element_type=F32
    )


def pick(value, index, axis=0):
    return lax.dynamic_index_in_dim(value, index, axis, keepdims=False)


def after(value, earlier):
    cols, width = value.shape[-1], earlier.shape[-1]
    row = earlier[(0,) * (earlier.ndim - 1)]
    row = jnp.tile(row, cols // width) if cols > width else row[:cols]
    return value + (0.0 * row.astype(F32)).astype(value.dtype)


def encode(value, gain):
    return (value * (lax.rsqrt(jnp.maximum(jnp.abs(value), 1e-35)) * gain)).astype(F16)


def decode(code, gain):
    code = code.astype(F32)
    return code * jnp.abs(code) * (1.0 / (gain * gain))


MOST_GRAD, MOST_PROJ, MOST_TARGET = 16.0, 48.0, 480.0
NORM_GAIN = 0.5


def gain_for(most):
    return 2.0 ** math.floor(15.99 - 0.5 * math.log2(most))


def per_device(n_p, n_g, grads, proj_matrix, targets):
    n_z = n_p // 2
    p, g = lax.axis_index("proj"), lax.axis_index("grp")
    py, pz = p % 2, p // 2
    rows = grads.shape[0]
    width = proj_matrix.shape[1]
    tgt_rows = targets.shape[0]
    own = rows * n_g // n_p
    piece = width // n_z
    half = rows // 2

    most_feature = grads.shape[1] * n_p * MOST_GRAD * MOST_PROJ
    feature_gain = gain_for(most_feature)
    product_gain = gain_for(most_feature * MOST_TARGET * piece * n_g)

    z_bits = [1 << k for k in range(n_z.bit_length() - 1)]

    def reversed_bits(z):
        return sum(((z >> k) & 1) << (len(z_bits) - 1 - k) for k in range(len(z_bits)))

    last, flags = [None], {"gate": True, "mark": True}

    def then(value):
        return value if last[0] is None or not flags["gate"] else after(value, last[0])

    def done(value):
        if flags["mark"]:
            last[0] = value
        return value

    def step(work, *args, gate=True, mark=True):
        flags.update(gate=gate, mark=mark)
        return work(*args)

    def side(value, y):
        shape = (rows // (2 * own), 2, own) + value.shape[1:]
        return pick(value.reshape(shape), y, 1).reshape((half,) + value.shape[1:])

    order = sorted(range(n_z), key=lambda k: [k & bit for bit in z_bits])


    def columns(value):
        return jnp.stack([lax.dynamic_slice_in_dim(value, (pz ^ k) * piece, piece, 1) for k in order])

    kept, code, features = {}, {}, {}

    def partial_away(i, chunk):
        part = done(jnp.dot(then(side(chunk, 1 - py)), proj_matrix, preferred_element_type=F32))
        code[i] = swap(encode(part, feature_gain), "proj", n_p, 1)

    def partial_kept(i, chunk):
        kept[i] = done(jnp.dot(then(side(chunk, py)), proj_matrix, preferred_element_type=F32))

    def collect(i):
        return done(then(kept[i]) + decode(code[i], feature_gain))

    def spread(i, bit):
        part = collect(i)
        part = columns(part) if bit == 1 else part
        kept[i], away = jnp.split(part, 2)
        code[i] = swap(encode(away, feature_gain), "proj", n_p, 2 * bit)

    def finish(i):
        features[i] = collect(i)[0].astype(BF16)

    def targets_over_z(blocks, bit):
        blocks = then(blocks)
        low, high = jnp.split(blocks, 2, axis=2)
        upper = (pz // bit) % 2 == 1
        return jnp.where(upper, high, low), swap(jnp.where(upper, low, high), "proj", n_p, 2 * bit)

    def joined(keep, got):
        return done(jnp.concatenate([keep, then(got)]))

    grads_2 = swap(grads, "grp", n_g, 2)
    grads_1 = swap(grads, "grp", n_g, 1)

    step(partial_away, 0, grads)
    grads_3 = swap(grads_2, "grp", n_g, 1)
    tgt = step(targets_over_z, targets[None], z_bits[-1])
    step(partial_away, 1, grads_1)
    step(partial_kept, 0, grads)
    step(spread, 0, 1)
    step(partial_kept, 1, grads_1)
    step(partial_away, 2, grads_2)
    step(spread, 1, 1)
    step(partial_kept, 2, grads_2)
    for bit in z_bits[-2::-1]:
        tgt = step(targets_over_z, step(joined, *tgt), bit, gate=False)
    step(partial_away, 3, grads_3)
    step(partial_kept, 3, grads_3)
    step(spread, 2, 1)
    for bit in z_bits[1:]:
        step(spread, 0, bit, mark=False)
    tgt = step(joined, *tgt)
    other = swap(tgt, "proj", n_p, 1)
    for bit in z_bits[1:]:
        step(spread, 1, bit)
    step(finish, 0)
    step(spread, 3, 1, gate=False)
    for bit in z_bits[1:]:
        step(spread, 2, bit, gate=False)
    step(finish, 1)
    for bit in z_bits[1:]:
        step(spread, 3, bit)
    step(finish, 2)
    step(finish, 3)

    in_chunk = n_z // n_g

    def row_block(z):
        return pick(features, ((z // in_chunk) ^ g) * in_chunk + z % in_chunk)

    features = jnp.stack([features[i] for i in range(n_g)]).reshape(n_z, own, piece)
    features = jnp.stack([row_block(pz ^ k) for k in range(n_z)])
    feature_sq = jnp.sum(jnp.square(features.astype(F32)), axis=2)
    features = features.reshape(n_z * own, piece)

    def of_member(q, mine, partners):
        places = [reversed_bits(pz ^ ((g ^ q) * in_chunk + n)) for n in range(in_chunk)]
        return jnp.concatenate([pick(value, at) for at in places for value in (mine, partners)])

    def products_of(q):
        return inner_rows(features, of_member(q, tgt, other)).reshape(n_z, own, -1)

    far, near = slice(1, n_z), slice(0, 1)
    prods = {3: products_of(3)}
    got_3 = swap(done(prods[3]), "grp", n_g, 1)
    prods[2] = products_of(2)
    prods[1] = products_of(1)
    got_1 = swap(then(prods[1]), "grp", n_g, 1)
    prods[0] = products_of(0)
    far_part = prods[2] + got_3
    own_part = prods[0] + got_1

    tgt_sq = [jnp.sum(jnp.square(value.astype(F32)), axis=2) for value in (tgt, other)]
    tgt_sq = jnp.stack([of_member(q, *tgt_sq) for q in range(n_g)])
    cols = tgt_sq.shape[1]
    got = swap(jnp.concatenate([feature_sq.reshape(-1), tgt_sq[1], tgt_sq[3]]), "grp", n_g, 1)
    feature_sq = feature_sq + got[: n_z * own].reshape(n_z, own)
    tgt_sq = [tgt_sq[2 * n] + got[n_z * own + n * cols :][:cols] for n in range(2)]

    def norm_rows(feature_sq, tgt_sq):
        rows = jnp.concatenate([jnp.pad(feature_sq, ((0, 0), (0, cols - own))), tgt_sq[None]])
        return jnp.pad(rows, ((0, -rows.shape[0] % 8), (0, 0)))

    def coded(product, norms):
        return jnp.concatenate([encode(product, product_gain), encode(jnp.sqrt(norms), NORM_GAIN)])

    def decoded(code, rows):
        product, norms = jnp.split(code, [rows])
        return decode(product, product_gain), jnp.square(decode(norms, NORM_GAIN))

    far_rows = (n_z - 1) * own
    codes = [swap(coded(far_part[far].reshape(far_rows, cols), norm_rows(feature_sq, tgt_sq[1])), "grp", n_g, 2)]
    codes.append(swap(encode(far_part[near][0], product_gain), "grp", n_g, 2))
    got, got_norms = decoded(codes[0], far_rows)
    part = done(then(own_part[far]) + got.reshape(n_z - 1, own, cols))
    feature_sq = feature_sq + got_norms[:n_z, :own]
    tgt_sq = tgt_sq[0] + got_norms[n_z]

    norms = [norm_rows(feature_sq[k : k + 1], tgt_sq) for k in range(n_z)]
    sends = [swap(coded(part[k - 1], norms[k]), "proj", n_p, 2 * k) for k in range(n_z - 1, 0, -1)]
    total = then(own_part[near])[0] + decode(codes[1], product_gain)
    norms = norms[0]
    for code in sends:
        got, got_norms = decoded(code, own)
        total, norms = total + got, norms + got_norms

    factor = float(width * n_g) ** 0.5
    scores = factor * total * lax.rsqrt(norms[0, :own] + EPS)[:, None] * lax.rsqrt(norms[1] + EPS)[None, :]
    blocks = jnp.split(scores, 2 * in_chunk, axis=1)
    swapped = jnp.concatenate([blocks[n ^ 1] for n in range(2 * in_chunk)], axis=1)
    return jnp.where(py == 0, scores, swapped)


def solution(mesh):
    n_p, n_g = mesh.shape["proj"], mesh.shape["grp"]

    def body(grads, proj_matrix, targets):
        return per_device(n_p, n_g, grads, proj_matrix, targets)

    placed = (P("grp", "proj"), P("proj", "grp"), P("proj", "grp"))
    return jax.shard_map(
        body, mesh=mesh, in_specs=placed, out_specs=P("proj", "grp"), check_vma=False
    )
```
